32 devices in a mesh: ty: 8 (over z, x), tx: 4 (over y, core).
Axes of the slice: x: 2, y: 2, z: 4, core: 2. Of those that a mesh axis runs over, the one named last changes fastest.
Arguments:
- fields: bfloat16 [2, 48, 64, 4096], P(None, None, 'ty', 'tx'), may hold values from -6 to 6
- kernel_one: bfloat16 [3, 3, 48, 32], replicated, may hold values from -0.3125 to 0.3125
- bias_one: float32 [32], replicated, may hold values from -1.5 to 1.5
- kernel_two: bfloat16 [3, 3, 32, 64], replicated, may hold values from -0.75 to 0.75
- bias_two: float32 [64], replicated, may hold values from -1.5 to 1.5
- kernel_three: bfloat16 [3, 3, 64, 128], replicated, may hold values from -0.5 to 0.5
- bias_three: float32 [128], replicated, may hold values from -1.5 to 1.5
- kernel_coarse: bfloat16 [3, 3, 128, 256], replicated, may hold values from -0.375 to 0.375
- bias_coarse: float32 [256], replicated, may hold values from -1.5 to 1.5
- decode_three: bfloat16 [3, 3, 384, 128], replicated, may hold values from -0.15625 to 0.15625
- offset_three: float32 [128], replicated, may hold values from -1.5 to 1.5
- decode_two: bfloat16 [3, 3, 192, 64], replicated, may hold values from -0.21875 to 0.21875
- offset_two: float32 [64], replicated, may hold values from -1.5 to 1.5
- decode_one: bfloat16 [3, 3, 96, 32], replicated, may hold values from -0.3125 to 0.3125
- offset_one: float32 [32], replicated, may hold values from -1.5 to 1.5
- head_kernel: bfloat16 [32, 48], replicated, may hold values from -1 to 1
- head_offset: float32 [48], replicated, may hold values from -3 to 3
Outputs:
- corrected: float32 [2, 48, 64, 4096], P(None, None, 'ty', 'tx')
The draws below stay inside these ranges and needn't reach their ends.
All inputs are finite; a program needn't handle non-finite values.
Results may differ from the reference program's by a relative error of at most 0.009.
Values may be sent and summed in bfloat16 or wider, within the bound.
A program may use at most 128 MiB of HBM per device.

```python
import jax
import jax.numpy as jnp
from jax import lax

VARS = 48
C1 = 32
C2 = 64
C3 = 128
C4 = 256
HOURS = 2
NY = 64
NX = 4096


def steps_of(key, shape, shards, low, high):
    level, own = 1.0, jax.random.fold_in(key, 6)
    for axis_at, blocks in shards:
        heights = jnp.exp(jax.random.uniform(jax.random.fold_in(own, axis_at), (blocks,), jnp.float32, low / len(shards), high / len(shards)))
        level = level * jnp.repeat(heights, shape[axis_at] // blocks).reshape([-1 if axis == axis_at else 1 for axis in range(len(shape))])
    return level


def gaussian(rng, shape, deviation, limit, split=(), dtype=jnp.bfloat16):
    level = steps_of(rng, shape, split, -0.22, 0.18) if split else 1.0
    values = jax.random.normal(rng, shape, jnp.float32) * deviation * level
    return jnp.minimum(jnp.maximum(values, -limit), limit).astype(dtype)


def setup_inputs(seed: int = 0) -> dict:
    splits = jax.random.split(jax.random.key(seed), 18)
    fields = gaussian(splits[0], (HOURS, VARS, NY, NX), 1.0, 6.0, ((2, 8), (3, 4)))
    kernel_one = gaussian(splits[1], (3, 3, VARS, C1), (9 * VARS) ** -0.5, 0.3125)
    bias_one = gaussian(splits[2], (C1,), 0.25, 1.5, (), jnp.float32)
    kernel_two = gaussian(splits[3], (3, 3, C1, C2), (2 * C1) ** -0.5, 0.75)
    bias_two = gaussian(splits[4], (C2,), 0.25, 1.5, (), jnp.float32)
    kernel_three = gaussian(splits[5], (3, 3, C2, C3), (2 * C2) ** -0.5, 0.5)
    bias_three = gaussian(splits[6], (C3,), 0.25, 1.5, (), jnp.float32)
    kernel_coarse = gaussian(splits[7], (3, 3, C3, C4), (2 * C3) ** -0.5, 0.375)
    bias_coarse = gaussian(splits[8], (C4,), 0.25, 1.5, (), jnp.float32)
    decode_three = gaussian(splits[9], (3, 3, C4 + C3, C3), (4 * (C4 + C3)) ** -0.5, 0.15625)
    offset_three = gaussian(splits[10], (C3,), 0.25, 1.5, (), jnp.float32)
    decode_two = gaussian(splits[11], (3, 3, C3 + C2, C2), (4 * (C3 + C2)) ** -0.5, 0.21875)
    offset_two = gaussian(splits[12], (C2,), 0.25, 1.5, (), jnp.float32)
    decode_one = gaussian(splits[13], (3, 3, C2 + C1, C1), (4 * (C2 + C1)) ** -0.5, 0.3125)
    offset_one = gaussian(splits[14], (C1,), 0.25, 1.5, (), jnp.float32)
    head_kernel = gaussian(splits[15], (C1, VARS), C1 ** -0.5, 1.0)
    head_offset = gaussian(splits[16], (VARS,), 0.5, 3.0, (), jnp.float32)
    return dict(fields=fields, kernel_one=kernel_one, bias_one=bias_one, kernel_two=kernel_two, bias_two=bias_two, kernel_three=kernel_three, bias_three=bias_three, kernel_coarse=kernel_coarse, bias_coarse=bias_coarse, decode_three=decode_three, offset_three=offset_three, decode_two=decode_two, offset_two=offset_two, decode_one=decode_one, offset_one=offset_one, head_kernel=head_kernel, head_offset=head_offset)


def convolve(tensor, kernel, offset):
    result = lax.conv_general_dilated(tensor, kernel, (1, 1), ((1, 1), (1, 1)), dimension_numbers=("NCHW", "HWIO", "NCHW"), preferred_element_type=jnp.float32)
    return jax.nn.silu(result + offset[None, :, None, None]).astype(jnp.bfloat16)


def average_pool(tensor):
    shape = tensor.shape
    blocks = tensor.astype(jnp.float32).reshape(shape[0], shape[1], shape[2] // 2, 2, shape[3] // 2, 2)
    return jnp.mean(blocks, axis=(3, 5)).astype(jnp.bfloat16)


def upsample(tensor):
    return jnp.repeat(jnp.repeat(tensor, 2, axis=2), 2, axis=3)


def reference(fields, kernel_one, bias_one, kernel_two, bias_two, kernel_three, bias_three, kernel_coarse, bias_coarse, decode_three, offset_three, decode_two, offset_two, decode_one, offset_one, head_kernel, head_offset):
    skip_one = convolve(fields, kernel_one, bias_one)
    skip_two = convolve(average_pool(skip_one), kernel_two, bias_two)
    skip_three = convolve(average_pool(skip_two), kernel_three, bias_three)
    coarse = convolve(average_pool(skip_three), kernel_coarse, bias_coarse)
    back_three = convolve(jnp.concatenate([upsample(coarse), skip_three], axis=1), decode_three, offset_three)
    back_two = convolve(jnp.concatenate([upsample(back_three), skip_two], axis=1), decode_two, offset_two)
    back_one = convolve(jnp.concatenate([upsample(back_two), skip_one], axis=1), decode_one, offset_one)
    projected = jnp.einsum("bchw,cv->bvhw", back_one.astype(jnp.float32), head_kernel.astype(jnp.float32), precision=lax.Precision.HIGHEST)
    return fields.astype(jnp.float32) + head_offset[None, :, None, None] + projected
```

```python
import functools

import jax
import jax.numpy as jnp
from jax import lax
from jax.experimental import pallas as pl
from jax.experimental.pallas import tpu as pltpu
from jax.sharding import PartitionSpec as P

LANES = 128
MESH = pl.DeviceIdType.MESH


def halved(width):
    return -(-width // (2 * LANES)) * LANES


def kernel(
    sizes,
    fields,
    k1,
    k2,
    k3,
    kc,
    d3,
    d2,
    d1,
    hk,
    bias,
    out,
    f0,
    s1,
    p1,
    s2,
    p2,
    s3,
    p3,
    c4,
    u3,
    b3,
    u2,
    b2,
    u1,
    pool_m,
    up_m,
    send,
    recv,
):
    nty, ntx, offsets = sizes
    hours, rows, _, core = fields.shape
    ty, tx = lax.axis_index("ty"), lax.axis_index("tx")
    has_up, has_down = ty > 0, ty < nty - 1
    has_left, has_right = tx > 0, tx < ntx - 1
    far = LANES + core

    for buf in (f0, s1, p1, s2, p2, s3, p3, c4, b3, b2):
        edge = jnp.zeros((buf.shape[0],) + buf.shape[2:], buf.dtype)
        buf[:, 0] = edge
        buf[:, buf.shape[1] - 1] = edge
    side = jnp.zeros((hours, rows) + (f0.shape[2], LANES), f0.dtype)
    f0[:, 1 : rows + 1, :, 0:LANES] = side
    f0[:, 1 : rows + 1, :, far : far + LANES] = side

    barrier = pltpu.get_barrier_semaphore()
    sides = (
        (has_up, {"ty": ty - 1}),
        (has_down, {"ty": ty + 1}),
        (has_left, {"tx": tx - 1}),
        (has_right, {"tx": tx + 1}),
    )
    count = jnp.int32(0)
    for has, where in sides:
        count = count + jnp.where(has, 1, 0)

        @pl.when(has)
        def _():
            pl.semaphore_signal(barrier, inc=1, device_id=where, device_id_type=MESH)

    pl.semaphore_wait(barrier, count)

    def pair(slot, first, second):
        made = []
        for at, (has, other, where, src, dst) in enumerate((first, second)):
            copy = pltpu.make_async_remote_copy(
                src_ref=src,
                dst_ref=dst,
                send_sem=send.at[slot * 2 + at],
                recv_sem=recv.at[slot * 2 + at],
                device_id=where,
                device_id_type=MESH,
            )
            made.append((has, other, copy))

            @pl.when(has)
            def _():
                copy.start()

        def wait():
            for has, other, copy in made:

                @pl.when(has)
                def _():
                    copy.wait_send()

                @pl.when(other)
                def _():
                    copy.wait_recv()

        return wait

    def vertical(slot, top, bottom, after, before):
        return pair(
            slot,
            (has_up, has_down, {"ty": ty - 1}, top, after),
            (has_down, has_up, {"ty": ty + 1}, bottom, before),
        )

    def row_exchange(slot, buf):
        last = buf.shape[1] - 1
        return vertical(slot, buf.at[:, 1], buf.at[:, last - 1], buf.at[:, last], buf.at[:, 0])

    middle = pl.ds(LANES, core)
    wait_sides = pair(
        0,
        (
            has_left,
            has_right,
            {"tx": tx - 1},
            fields.at[:, :, :, pl.ds(0, LANES)],
            f0.at[:, pl.ds(1, rows), :, pl.ds(far, LANES)],
        ),
        (
            has_right,
            has_left,
            {"tx": tx + 1},
            fields.at[:, :, :, pl.ds(core - LANES, LANES)],
            f0.at[:, pl.ds(1, rows), :, pl.ds(0, LANES)],
        ),
    )
    wait_rows = vertical(
        1,
        fields.at[:, 0],
        fields.at[:, rows - 1],
        f0.at[:, rows + 1, :, middle],
        f0.at[:, 0, :, middle],
    )

    f0[:, 1 : rows + 1, :, LANES:far] = fields[...]
    two, one = 2 * LANES, LANES
    tall = lax.broadcasted_iota(jnp.int32, (two, one), 0)
    wide = lax.broadcasted_iota(jnp.int32, (two, one), 1)
    pool_m[...] = jnp.where(lax.shift_right_logical(tall, 1) == wide, 0.25, 0.0).astype(jnp.bfloat16)
    tall = lax.broadcasted_iota(jnp.int32, (one, two), 0)
    wide = lax.broadcasted_iota(jnp.int32, (one, two), 1)
    up_m[...] = jnp.where(lax.shift_right_logical(wide, 1) == tall, 1.0, 0.0).astype(jnp.bfloat16)

    wait_sides()
    waits = []
    for at, start in enumerate((0, far)):
        lanes = pl.ds(start, LANES)
        waits.append(
            vertical(
                2 + at,
                f0.at[:, 1, :, lanes],
                f0.at[:, rows, :, lanes],
                f0.at[:, rows + 1, :, lanes],
                f0.at[:, 0, :, lanes],
            )
        )
    wait_rows()
    for wait in waits:
        wait()

    def inside(width, level):
        column = lax.broadcasted_iota(jnp.int32, (1, width), 1)
        column = column + (tx * (core >> level) - (LANES >> level))
        return (column >= 0) & (column < ntx * (core >> level))

    def conv(weights, at, operand, level):
        width = operand.shape[1]
        size = weights.shape[0] // 3
        terms = jnp.dot(weights[...], operand, preferred_element_type=jnp.float32)
        total = terms[size : 2 * size] + bias[offsets[at] : offsets[at] + size]
        total = total + pltpu.roll(terms[:size], 1, 1)
        total = total + pltpu.roll(terms[2 * size :], width - 1, 1)
        half = 0.5 * total
        result = half * jnp.tanh(half) + half
        if level is not None:
            result = jnp.where(inside(width, level), result, 0.0)
        return result.astype(jnp.bfloat16)

    def pooled(first, second):
        width = first.shape[1]
        pieces = []
        for start in range(0, width, two):
            stop = min(start + two, width)
            block = pool_m[0 : stop - start]
            pieces.append(
                jnp.dot(first[:, start:stop], block, preferred_element_type=jnp.float32)
                + jnp.dot(second[:, start:stop], block, preferred_element_type=jnp.float32)
            )
        return jnp.concatenate(pieces, axis=1).astype(jnp.bfloat16)

    def widen(src, dst):
        width = dst.shape[3]
        n = src.shape[1]

        def step(index, carry):
            h, r = lax.div(index, n), lax.rem(index, n)
            for start in range(0, width, two):
                stop = min(start + two, width)
                block = src[h, r, :, start // 2 : start // 2 + one]
                dst[h, r, :, start:stop] = jnp.dot(
                    block, up_m[:, 0 : stop - start], preferred_element_type=jnp.float32
                ).astype(jnp.bfloat16)
            return carry

        lax.fori_loop(0, hours * n, step, 0)

    def taps(buf, h, r):
        block = buf[h, pl.ds(r, 3)]
        return block.reshape(3 * buf.shape[2], buf.shape[3])

    def encode(src, weights, at, dst, nxt, level):
        half = (src.shape[1] - 2) // 2

        def step(index, carry):
            h, i = lax.div(index, half), lax.rem(index, half)
            made = []
            for off in range(2):
                r = 2 * i + off
                row = conv(weights, at, taps(src, h, r), level)
                dst[h, r + 1] = row
                made.append(row)
            nxt[h, i + 1] = pooled(*made)
            return carry

        lax.fori_loop(0, hours * half, step, 0)

    def decode(up, skip, weights, at, write, level):
        half = (skip.shape[1] - 2) // 2

        def step(index, carry):
            h, i = lax.div(index, half), lax.rem(index, half)
            above, here, below = up[h, i], up[h, i + 1], up[h, i + 2]
            for off in range(2):
                r = 2 * i + off
                three = (above, here, here) if off == 0 else (here, here, below)
                operand = jnp.concatenate(three + (taps(skip, h, r),), axis=0)
                write(h, r, conv(weights, at, operand, level))
            return carry

        lax.fori_loop(0, hours * half, step, 0)

    encode(f0, k1, 0, s1, p1, 0)
    wait_p1 = row_exchange(4, p1)
    wait_s1 = row_exchange(5, s1)
    wait_p1()
    encode(p1, k2, 1, s2, p2, 1)
    wait_p2 = row_exchange(6, p2)
    wait_s2 = row_exchange(7, s2)
    wait_p2()
    encode(p2, k3, 2, s3, p3, 2)
    wait_p3 = row_exchange(8, p3)
    wait_s3 = row_exchange(9, s3)
    wait_p3()
    for h in range(hours):
        for r in range(c4.shape[1] - 2):
            c4[h, r + 1] = conv(kc, 3, taps(p3, h, r), 3)
    wait_c4 = row_exchange(10, c4)
    wait_c4()
    wait_s3()
    widen(c4, u3)

    def keep(buf):
        def write(h, r, value):
            buf[h, r + 1] = value

        return write

    decode(u3, s3, d3, 4, keep(b3), 2)
    wait_b3 = row_exchange(11, b3)
    wait_b3()
    wait_s2()
    widen(b3, u2)
    decode(u2, s2, d2, 5, keep(b2), 1)
    wait_b2 = row_exchange(12, b2)
    wait_b2()
    wait_s1()
    widen(b2, u1)

    def head(h, r, value):
        total = jnp.dot(hk[...], value[:, LANES:far], preferred_element_type=jnp.float32)
        total = total + bias[offsets[7] : offsets[7] + hk.shape[0]]
        out[h, r] = total + f0[h, r + 1, :, LANES:far].astype(jnp.float32)

    decode(u1, s1, d1, 6, head, None)


def stacked(weights, parts):
    blocks = []
    for start, stop in parts:
        block = jnp.transpose(weights[:, :, start:stop], (1, 3, 0, 2))
        blocks.append(block.reshape(3 * weights.shape[3], 3 * (stop - start)))
    return blocks[0] if len(blocks) == 1 else jnp.concatenate(blocks, axis=1)


def body(
    nty,
    ntx,
    fields,
    kernel_one,
    bias_one,
    kernel_two,
    bias_two,
    kernel_three,
    bias_three,
    kernel_coarse,
    bias_coarse,
    decode_three,
    offset_three,
    decode_two,
    offset_two,
    decode_one,
    offset_one,
    head_kernel,
    head_offset,
):
    hours, nv, rows, core = fields.shape
    biases = (
        bias_one,
        bias_two,
        bias_three,
        bias_coarse,
        offset_three,
        offset_two,
        offset_one,
        head_offset,
    )
    offsets, total = [], 0
    for item in biases:
        offsets.append(total)
        total += item.shape[0]
    bias = jnp.concatenate(biases).reshape(total, 1)
    c1, c2, c3, c4 = (k.shape[3] for k in (kernel_one, kernel_two, kernel_three, kernel_coarse))
    encoders = [
        stacked(k, ((0, k.shape[2]),))
        for k in (kernel_one, kernel_two, kernel_three, kernel_coarse)
    ]
    decoders = [
        stacked(k, ((0, cut), (cut, k.shape[2])))
        for k, cut in ((decode_three, c4), (decode_two, c3), (decode_one, c2))
    ]
    w1 = core + 2 * LANES
    w2 = halved(w1)
    w3 = halved(w2)
    w4 = halved(w3)
    r1, r2, r3, r4 = (rows + 2, rows // 2 + 2, rows // 4 + 2, rows // 8 + 2)
    shapes = (
        (hours, r1, nv, w1),
        (hours, r1, c1, w1),
        (hours, r2, c1, w2),
        (hours, r2, c2, w2),
        (hours, r3, c2, w3),
        (hours, r3, c3, w3),
        (hours, r4, c3, w4),
        (hours, r4, c4, w4),
        (hours, r4, c4, w3),
        (hours, r3, c3, w3),
        (hours, r3, c3, w2),
        (hours, r2, c2, w2),
        (hours, r2, c2, w1),
        (2 * LANES, LANES),
        (LANES, 2 * LANES),
    )
    vmem = pl.BlockSpec(memory_space=pltpu.VMEM)
    result = pl.pallas_call(
        functools.partial(kernel, (nty, ntx, tuple(offsets))),
        out_shape=jax.ShapeDtypeStruct((hours, rows, nv, core), jnp.float32),
        in_specs=[vmem] * 10,
        out_specs=vmem,
        scratch_shapes=[pltpu.VMEM(shape, jnp.bfloat16) for shape in shapes]
        + [pltpu.SemaphoreType.DMA((26,)), pltpu.SemaphoreType.DMA((26,))],
        compiler_params=pltpu.CompilerParams(
            collective_id=0, has_side_effects=True, vmem_limit_bytes=56 * 2**20
        ),
    )(jnp.transpose(fields, (0, 2, 1, 3)), *encoders, *decoders, head_kernel.T, bias)
    return jnp.transpose(result, (0, 2, 1, 3))


def solution(mesh):
    return jax.shard_map(
        functools.partial(body, mesh.shape["ty"], mesh.shape["tx"]),
        mesh=mesh,
        in_specs=(P(None, None, "ty", "tx"),) + (P(),) * 16,
        out_specs=P(None, None, "ty", "tx"),
        check_vma=False,
    )
```

```python
import functools

import jax
import jax.numpy as jnp
from jax import lax
from jax.experimental import pallas as pl
from jax.experimental.pallas import tpu as pltpu
from jax.sharding import PartitionSpec as P

LANES = 128
MESH = pl.DeviceIdType.MESH


def halved(width):
    return -(-width // (2 * LANES)) * LANES


def kernel(
    sizes,
    fields,
    k1,
    o1,
    k2,
    o2,
    k3,
    o3,
    kc,
    oc,
    d3,
    e3,
    d2,
    e2,
    d1,
    e1,
    hk,
    he,
    out,
    f0,
    s1,
    p1,
    s2,
    p2,
    s3,
    p3,
    c4,
    u3,
    b3,
    u2,
    b2,
    u1,
    pool_m,
    up_m,
    w1,
    w2,
    w3,
    wc,
    x3,
    x2,
    x1,
    wh,
    v1,
    v2,
    v3,
    vc,
    y3,
    y2,
    y1,
    yh,
    send,
    recv,
):
    nty, ntx = sizes
    hours, rows, _, core = fields.shape
    ty, tx = lax.axis_index("ty"), lax.axis_index("tx")
    has_up, has_down = ty > 0, ty < nty - 1
    has_left, has_right = tx > 0, tx < ntx - 1
    far = LANES + core

    for buf in (f0, s1, p1, s2, p2, s3, p3, c4, b3, b2):
        edge = jnp.zeros((buf.shape[0],) + buf.shape[2:], buf.dtype)
        buf[:, 0] = edge
        buf[:, buf.shape[1] - 1] = edge
    side = jnp.zeros((hours, rows) + (f0.shape[2], LANES), f0.dtype)
    f0[:, 1 : rows + 1, :, 0:LANES] = side
    f0[:, 1 : rows + 1, :, far : far + LANES] = side

    barrier = pltpu.get_barrier_semaphore()
    sides = (
        (has_up, {"ty": ty - 1}),
        (has_down, {"ty": ty + 1}),
        (has_left, {"tx": tx - 1}),
        (has_right, {"tx": tx + 1}),
    )
    count = jnp.int32(0)
    for has, where in sides:
        count = count + jnp.where(has, 1, 0)

        @pl.when(has)
        def _():
            pl.semaphore_signal(barrier, inc=1, device_id=where, device_id_type=MESH)

    pl.semaphore_wait(barrier, count)

    def pair(slot, first, second):
        made = []
        for at, (has, other, where, src, dst) in enumerate((first, second)):
            copy = pltpu.make_async_remote_copy(
                src_ref=src,
                dst_ref=dst,
                send_sem=send.at[slot * 2 + at],
                recv_sem=recv.at[slot * 2 + at],
                device_id=where,
                device_id_type=MESH,
            )
            made.append((has, other, copy))

            @pl.when(has)
            def _():
                copy.start()

        def wait():
            for has, other, copy in made:

                @pl.when(has)
                def _():
                    copy.wait_send()

                @pl.when(other)
                def _():
                    copy.wait_recv()

        return wait

    def vertical(slot, top, bottom, after, before):
        return pair(
            slot,
            (has_up, has_down, {"ty": ty - 1}, top, after),
            (has_down, has_up, {"ty": ty + 1}, bottom, before),
        )

    def row_exchange(slot, buf):
        last = buf.shape[1] - 1
        return vertical(slot, buf.at[:, 1], buf.at[:, last - 1], buf.at[:, last], buf.at[:, 0])

    middle = pl.ds(LANES, core)
    wait_sides = pair(
        0,
        (
            has_left,
            has_right,
            {"tx": tx - 1},
            fields.at[:, :, :, pl.ds(0, LANES)],
            f0.at[:, pl.ds(1, rows), :, pl.ds(far, LANES)],
        ),
        (
            has_right,
            has_left,
            {"tx": tx + 1},
            fields.at[:, :, :, pl.ds(core - LANES, LANES)],
            f0.at[:, pl.ds(1, rows), :, pl.ds(0, LANES)],
        ),
    )
    wait_rows = vertical(
        1,
        fields.at[:, 0],
        fields.at[:, rows - 1],
        f0.at[:, rows + 1, :, middle],
        f0.at[:, 0, :, middle],
    )

    f0[:, 1 : rows + 1, :, LANES:far] = fields[...]
    two, one = 2 * LANES, LANES
    tall = lax.broadcasted_iota(jnp.int32, (two, one), 0)
    wide = lax.broadcasted_iota(jnp.int32, (two, one), 1)
    pool_m[...] = jnp.where(lax.shift_right_logical(tall, 1) == wide, 0.25, 0.0).astype(jnp.bfloat16)
    tall = lax.broadcasted_iota(jnp.int32, (one, two), 0)
    wide = lax.broadcasted_iota(jnp.int32, (one, two), 1)
    up_m[...] = jnp.where(lax.shift_right_logical(wide, 1) == tall, 1.0, 0.0).astype(jnp.bfloat16)

    def eye(n):
        down = lax.broadcasted_iota(jnp.int32, (n, n), 0)
        across = lax.broadcasted_iota(jnp.int32, (n, n), 1)
        return down == across

    def turned(block):
        return lax.dot_general(
            jnp.where(eye(block.shape[1]), 1.0, 0.0).astype(jnp.bfloat16),
            block,
            (((1,), (1,)), ((), ())),
            preferred_element_type=jnp.float32,
        ).astype(jnp.bfloat16)

    def arrange(src, dst, cuts):
        size = src.shape[3]
        count = dst.shape[0] // (3 * size)
        for off in range(count):
            for c in range(3):
                blocks = []
                for start, stop in cuts:
                    zero = jnp.zeros((stop - start, size), jnp.bfloat16)
                    taken = src[:, c, start:stop].reshape(3 * (stop - start), size)
                    blocks += [zero] * off + [taken] + [zero] * (count - 1 - off)
                block = blocks[0] if len(blocks) == 1 else jnp.concatenate(blocks, axis=0)
                at = (off * 3 + c) * size
                dst[at : at + size] = turned(block)

    def upright(src, dst):
        n = src.shape[0]
        row = jnp.broadcast_to(src[...].reshape(1, n), (n, n))
        dst[...] = jnp.sum(jnp.where(eye(n), row, 0.0), axis=1, keepdims=True)

    for src, dst in ((k1, w1), (k2, w2), (k3, w3), (kc, wc)):
        arrange(src, dst, ((0, src.shape[2]),))
    for src, dst, low in ((d3, x3, c4), (d2, x2, b3), (d1, x1, b2)):
        arrange(src, dst, ((0, low.shape[2]), (low.shape[2], src.shape[2])))
    wh[...] = turned(hk[...])
    for src, dst in zip((o1, o2, o3, oc, e3, e2, e1, he), (v1, v2, v3, vc, y3, y2, y1, yh)):
        upright(src, dst)

    wait_sides()
    waits = []
    for at, start in enumerate((0, far)):
        lanes = pl.ds(start, LANES)
        waits.append(
            vertical(
                2 + at,
                f0.at[:, 1, :, lanes],
                f0.at[:, rows, :, lanes],
                f0.at[:, rows + 1, :, lanes],
                f0.at[:, 0, :, lanes],
            )
        )
    wait_rows()
    for wait in waits:
        wait()

    def inside(width, level):
        column = lax.broadcasted_iota(jnp.int32, (1, width), 1)
        column = column + (tx * (core >> level) - (LANES >> level))
        return (column >= 0) & (column < ntx * (core >> level))

    def conv(weights, offset, operand, level):
        width = operand.shape[1]
        size = offset.shape[0]
        terms = jnp.dot(weights[...], operand, preferred_element_type=jnp.float32)
        made = []
        for at in range(0, terms.shape[0], 3 * size):
            total = terms[at + size : at + 2 * size] + offset[...]
            total = total + pltpu.roll(terms[at : at + size], 1, 1)
            total = total + pltpu.roll(terms[at + 2 * size : at + 3 * size], width - 1, 1)
            half = 0.5 * total
            result = half * jnp.tanh(half) + half
            if level is not None:
                result = jnp.where(inside(width, level), result, 0.0)
            made.append(result.astype(jnp.bfloat16))
        return made

    def pooled(values):
        width = values[0].shape[1]
        size = values[0].shape[0]
        tall = jnp.concatenate(values, axis=0)
        pieces = []
        for start in range(0, width, two):
            stop = min(start + two, width)
            pieces.append(
                jnp.dot(tall[:, start:stop], pool_m[0 : stop - start], preferred_element_type=jnp.float32)
            )
        sums = jnp.concatenate(pieces, axis=1)
        return [
            (sums[at : at + size] + sums[at + size : at + 2 * size]).astype(jnp.bfloat16)
            for at in range(0, size * len(values), 2 * size)
        ]

    def widen(src, dst, first, last):
        width = dst.shape[3]
        size = src.shape[2]
        n = last - first
        for start in range(0, width, two):
            stop = min(start + two, width)
            block = src[:, first:last, :, start // 2 : start // 2 + one]
            wide = jnp.dot(
                block.reshape(hours * n * size, one),
                up_m[:, 0 : stop - start],
                preferred_element_type=jnp.float32,
            ).astype(jnp.bfloat16)
            dst[:, first:last, :, start:stop] = wide.reshape(hours, n, size, stop - start)

    def taps(buf, h, r, n):
        block = buf[h, pl.ds(r, n)]
        return block.reshape(n * buf.shape[2], buf.shape[3])

    def edges(half, step):
        if half == 1:
            step(0)
            return

        def both(j, carry):
            step(j * (half - 1))
            return carry

        lax.fori_loop(0, 2, both, 0)

    def interior(half, step):
        def one_pair(j, carry):
            step(j)
            return carry

        if half > 2:
            lax.fori_loop(1, half - 1, one_pair, 0)

    def encode(src, weights, offset, dst, nxt, level, slot):
        half = (src.shape[1] - 2) // 2

        def step(i):
            made = []
            for h in range(hours):
                pair_of = conv(weights, offset, taps(src, h, 2 * i, 4), level)
                for off, row in enumerate(pair_of):
                    dst[h, 2 * i + off + 1] = row
                made += pair_of
            for h, row in enumerate(pooled(made)):
                nxt[h, i + 1] = row

        edges(half, step)
        waits = row_exchange(slot, nxt), row_exchange(slot + 1, dst)
        interior(half, step)
        return waits

    def decode(low, up, skip, weights, offset, write, level, wait):
        half = (skip.shape[1] - 2) // 2
        last = low.shape[1] - 1

        def step(i):
            for h in range(hours):
                above, here, below = up[h, i], up[h, i + 1], up[h, i + 2]
                operand = jnp.concatenate(
                    (above, here, here, below, taps(skip, h, 2 * i, 4)), axis=0
                )
                for off, row in enumerate(conv(weights, offset, operand, level)):
                    write(h, 2 * i + off, row)

        widen(low, up, 1, last)
        interior(half, step)
        wait()
        widen(low, up, 0, 1)
        widen(low, up, last, last + 1)
        edges(half, step)

    wait_p1, wait_s1 = encode(f0, w1, v1, s1, p1, 0, 4)
    wait_p1()
    wait_p2, wait_s2 = encode(p1, w2, v2, s2, p2, 1, 6)
    wait_p2()
    wait_p3, wait_s3 = encode(p2, w3, v3, s3, p3, 2, 8)
    wait_p3()
    for h in range(hours):
        for r in range(c4.shape[1] - 2):
            (c4[h, r + 1],) = conv(wc, vc, taps(p3, h, r, 3), 3)
    wait_c4 = row_exchange(10, c4)
    wait_s3()

    def keep(buf):
        def write(h, r, value):
            buf[h, r + 1] = value

        return write

    decode(c4, u3, s3, x3, y3, keep(b3), 2, wait_c4)
    wait_b3 = row_exchange(11, b3)
    wait_s2()
    decode(b3, u2, s2, x2, y2, keep(b2), 1, wait_b3)
    wait_b2 = row_exchange(12, b2)
    wait_s1()

    def head(h, r, value):
        total = jnp.dot(wh[...], value[:, LANES:far], preferred_element_type=jnp.float32)
        total = total + yh[...]
        out[h, r] = total + f0[h, r + 1, :, LANES:far].astype(jnp.float32)

    decode(b2, u1, s1, x1, y1, head, None, wait_b2)


def body(nty, ntx, fields, *weights):
    hours, nv, rows, core = fields.shape
    sizes = [k.shape[3] for k in weights[0:8:2]]
    c1, c2, c3, c4 = sizes
    w1 = core + 2 * LANES
    w2 = halved(w1)
    w3 = halved(w2)
    w4 = halved(w3)
    r1, r2, r3, r4 = (rows + 2, rows // 2 + 2, rows // 4 + 2, rows // 8 + 2)
    shapes = (
        (hours, r1, nv, w1),
        (hours, r1, c1, w1),
        (hours, r2, c1, w2),
        (hours, r2, c2, w2),
        (hours, r3, c2, w3),
        (hours, r3, c3, w3),
        (hours, r4, c3, w4),
        (hours, r4, c4, w4),
        (hours, r4, c4, w3),
        (hours, r3, c3, w3),
        (hours, r3, c3, w2),
        (hours, r2, c2, w2),
        (hours, r2, c2, w1),
        (2 * LANES, LANES),
        (LANES, 2 * LANES),
        (6 * c1, 4 * nv),
        (6 * c2, 4 * c1),
        (6 * c3, 4 * c2),
        (3 * c4, 3 * c3),
        (6 * c3, 4 * (c4 + c3)),
        (6 * c2, 4 * (c3 + c2)),
        (6 * c1, 4 * (c2 + c1)),
        (nv, c1),
    )
    columns = (c1, c2, c3, c4, c3, c2, c1, nv)
    vmem = pl.BlockSpec(memory_space=pltpu.VMEM)
    result = pl.pallas_call(
        functools.partial(kernel, (nty, ntx)),
        out_shape=jax.ShapeDtypeStruct((hours, rows, nv, core), jnp.float32),
        in_specs=[vmem] * 17,
        out_specs=vmem,
        scratch_shapes=[pltpu.VMEM(shape, jnp.bfloat16) for shape in shapes]
        + [pltpu.VMEM((n, 1), jnp.float32) for n in columns]
        + [pltpu.SemaphoreType.DMA((26,)), pltpu.SemaphoreType.DMA((26,))],
        compiler_params=pltpu.CompilerParams(
            collective_id=0, has_side_effects=True, vmem_limit_bytes=56 * 2**20
        ),
    )(jnp.transpose(fields, (0, 2, 1, 3)), *weights)
    return jnp.transpose(result, (0, 2, 1, 3))


def solution(mesh):
    return jax.shard_map(
        functools.partial(body, mesh.shape["ty"], mesh.shape["tx"]),
        mesh=mesh,
        in_specs=(P(None, None, "ty", "tx"),) + (P(),) * 16,
        out_specs=P(None, None, "ty", "tx"),
        check_vma=False,
    )
```

```python
import functools

import jax
import jax.numpy as jnp
from jax import lax
from jax.experimental import pallas as pl
from jax.experimental.pallas import tpu as pltpu
from jax.sharding import PartitionSpec as P

LANES = 128
MESH = pl.DeviceIdType.MESH


def halved(width):
    return -(-width // (2 * LANES)) * LANES


def kernel(
    sizes,
    fields,
    k1,
    o1,
    k2,
    o2,
    k3,
    o3,
    kc,
    oc,
    d3,
    e3,
    d2,
    e2,
    d1,
    e1,
    hk,
    he,
    out,
    f0,
    s1,
    p1,
    s2,
    p2,
    s3,
    p3,
    c4,
    u3,
    b3,
    u2,
    b2,
    u1,
    pool_m,
    up_m,
    w1,
    w2,
    w3,
    wc,
    x3,
    x2,
    x1,
    wh,
    v1,
    v2,
    v3,
    vc,
    y3,
    y2,
    y1,
    yh,
    q3,
    g3,
    q2,
    g2,
    q1,
    g1,
    send,
    recv,
):
    nty, ntx = sizes
    hours, rows, _, core = fields.shape
    ty, tx = lax.axis_index("ty"), lax.axis_index("tx")
    has_up, has_down = ty > 0, ty < nty - 1
    has_left, has_right = tx > 0, tx < ntx - 1
    far = LANES + core

    for buf in (f0, s1, p1, s2, p2, s3, p3, u3, u2, u1):
        edge = jnp.zeros((buf.shape[0],) + buf.shape[2:], buf.dtype)
        buf[:, 0] = edge
        buf[:, buf.shape[1] - 1] = edge
    for buf in (g3, g2, g1):
        buf[...] = jnp.zeros(buf.shape, buf.dtype)
    side = jnp.zeros((hours, rows) + (f0.shape[2], LANES), f0.dtype)
    f0[:, 1 : rows + 1, :, 0:LANES] = side
    f0[:, 1 : rows + 1, :, far : far + LANES] = side

    barrier = pltpu.get_barrier_semaphore()
    sides = (
        (has_up, {"ty": ty - 1}),
        (has_down, {"ty": ty + 1}),
        (has_left, {"tx": tx - 1}),
        (has_right, {"tx": tx + 1}),
    )
    count = jnp.int32(0)
    for has, where in sides:
        count = count + jnp.where(has, 1, 0)

        @pl.when(has)
        def _():
            pl.semaphore_signal(barrier, inc=1, device_id=where, device_id_type=MESH)

    pl.semaphore_wait(barrier, count)

    def pair(slot, first, second):
        made = []
        for at, (has, other, where, src, dst) in enumerate((first, second)):
            copy = pltpu.make_async_remote_copy(
                src_ref=src,
                dst_ref=dst,
                send_sem=send.at[slot * 2 + at],
                recv_sem=recv.at[slot * 2 + at],
                device_id=where,
                device_id_type=MESH,
            )
            made.append((has, other, copy))

            @pl.when(has)
            def _():
                copy.start()

        def wait():
            for has, other, copy in made:

                @pl.when(has)
                def _():
                    copy.wait_send()

                @pl.when(other)
                def _():
                    copy.wait_recv()

        return wait

    def vertical(slot, top, bottom, after, before):
        return pair(
            slot,
            (has_up, has_down, {"ty": ty - 1}, top, after),
            (has_down, has_up, {"ty": ty + 1}, bottom, before),
        )

    def row_exchange(slot, buf):
        last = buf.shape[1] - 1
        return vertical(slot, buf.at[:, 1], buf.at[:, last - 1], buf.at[:, last], buf.at[:, 0])

    middle = pl.ds(LANES, core)
    wait_sides = pair(
        0,
        (
            has_left,
            has_right,
            {"tx": tx - 1},
            fields.at[:, :, :, pl.ds(0, LANES)],
            f0.at[:, pl.ds(1, rows), :, pl.ds(far, LANES)],
        ),
        (
            has_right,
            has_left,
            {"tx": tx + 1},
            fields.at[:, :, :, pl.ds(core - LANES, LANES)],
            f0.at[:, pl.ds(1, rows), :, pl.ds(0, LANES)],
        ),
    )
    wait_rows = vertical(
        1,
        fields.at[:, 0],
        fields.at[:, rows - 1],
        f0.at[:, rows + 1, :, middle],
        f0.at[:, 0, :, middle],
    )

    f0[:, 1 : rows + 1, :, LANES:far] = fields[...]
    two, one = 2 * LANES, LANES
    tall = lax.broadcasted_iota(jnp.int32, (two, one), 0)
    wide = lax.broadcasted_iota(jnp.int32, (two, one), 1)
    pool_m[...] = jnp.where(lax.shift_right_logical(tall, 1) == wide, 0.25, 0.0).astype(jnp.bfloat16)
    tall = lax.broadcasted_iota(jnp.int32, (one, two), 0)
    wide = lax.broadcasted_iota(jnp.int32, (one, two), 1)
    up_m[...] = jnp.where(lax.shift_right_logical(wide, 1) == tall, 1.0, 0.0).astype(jnp.bfloat16)

    def eye(n):
        down = lax.broadcasted_iota(jnp.int32, (n, n), 0)
        across = lax.broadcasted_iota(jnp.int32, (n, n), 1)
        return down == across

    def turned(block):
        return lax.dot_general(
            jnp.where(eye(block.shape[1]), 1.0, 0.0).astype(jnp.bfloat16),
            block,
            (((1,), (1,)), ((), ())),
            preferred_element_type=jnp.float32,
        ).astype(jnp.bfloat16)

    def arrange(src, dst, cuts):
        straight = src.shape[2] == cuts[-1][1]
        size = src.shape[3] if straight else src.shape[2]
        count = dst.shape[0] // (3 * size)
        for c in range(3):
            if straight:
                rows_of = src[:, c]
            else:
                rows_of = jnp.stack([turned(src[a, c]) for a in range(3)])
            for off in range(count):
                blocks = []
                for start, stop in cuts:
                    zero = jnp.zeros((stop - start, size), jnp.bfloat16)
                    taken = rows_of[:, start:stop].reshape(3 * (stop - start), size)
                    blocks += [zero] * off + [taken] + [zero] * (count - 1 - off)
                block = blocks[0] if len(blocks) == 1 else jnp.concatenate(blocks, axis=0)
                at = (off * 3 + c) * size
                dst[at : at + size] = turned(block)

    def upright(src, dst):
        n = src.shape[0]
        row = jnp.broadcast_to(src[...].reshape(1, n), (n, n))
        dst[...] = jnp.sum(jnp.where(eye(n), row, 0.0), axis=1, keepdims=True)

    for src, dst, buf in ((k1, w1, f0), (k2, w2, p1), (k3, w3, p2), (kc, wc, p3)):
        arrange(src, dst, ((0, buf.shape[2]),))
    for src, dst, low, skip in ((d3, x3, c4, s3), (d2, x2, b3, s2), (d1, x1, b2, s1)):
        cut = low.shape[2]
        arrange(src, dst, ((0, cut), (cut, cut + skip.shape[2])))
    wh[...] = turned(hk[...])
    for src, dst in zip((o1, o2, o3, oc, e3, e2, e1, he), (v1, v2, v3, vc, y3, y2, y1, yh)):
        upright(src, dst)

    wait_sides()
    waits = []
    for at, start in enumerate((0, far)):
        lanes = pl.ds(start, LANES)
        waits.append(
            vertical(
                2 + at,
                f0.at[:, 1, :, lanes],
                f0.at[:, rows, :, lanes],
                f0.at[:, rows + 1, :, lanes],
                f0.at[:, 0, :, lanes],
            )
        )
    wait_rows()
    for wait in waits:
        wait()

    def inside(width, level):
        column = lax.broadcasted_iota(jnp.int32, (1, width), 1)
        column = column + (tx * (core >> level) - (LANES >> level))
        return (column >= 0) & (column < ntx * (core >> level))

    def combined(weights, size, operand, lanes):
        width = operand.shape[1]
        terms = jnp.dot(weights[...], operand, preferred_element_type=jnp.float32)
        made = []
        for at in range(0, terms.shape[0], 3 * size):
            total = terms[at + size : at + 2 * size]
            total = total + pltpu.roll(terms[at : at + size], 1, 1)
            total = total + pltpu.roll(terms[at + 2 * size : at + 3 * size], width - 1, 1)
            made.append(total if lanes is None else total[:, lanes[0] : lanes[1]])
        return made

    def conv(weights, offset, operand, level, lanes=None, more=(None, None)):
        made = []
        for total, extra in zip(combined(weights, offset.shape[0], operand, lanes), more):
            total = total + offset[...]
            if extra is not None:
                total = total + extra.astype(jnp.float32)
            half = 0.5 * total
            result = half * jnp.tanh(half) + half
            if level is not None:
                result = jnp.where(inside(result.shape[1], level), result, 0.0)
            made.append(result.astype(jnp.bfloat16))
        return made

    def pooled(values):
        width = values[0].shape[1]
        size = values[0].shape[0]
        tall = jnp.concatenate(values, axis=0)
        pieces = []
        for start in range(0, width, two):
            stop = min(start + two, width)
            pieces.append(
                jnp.dot(tall[:, start:stop], pool_m[0 : stop - start], preferred_element_type=jnp.float32)
            )
        sums = jnp.concatenate(pieces, axis=1)
        return [
            (sums[at : at + size] + sums[at + size : at + 2 * size]).astype(jnp.bfloat16)
            for at in range(0, size * len(values), 2 * size)
        ]

    def widen(src, dst, first, last):
        width = dst.shape[3]
        size = src.shape[2]
        n = last - first
        for start in range(0, width, two):
            stop = min(start + two, width)
            block = src[:, first:last, :, start // 2 : start // 2 + one]
            wide = jnp.dot(
                block.reshape(hours * n * size, one),
                up_m[:, 0 : stop - start],
                preferred_element_type=jnp.float32,
            ).astype(jnp.bfloat16)
            dst[:, first:last, :, start:stop] = wide.reshape(hours, n, size, stop - start)

    def taps(buf, h, r, n):
        block = buf[h, pl.ds(r, n)]
        return block.reshape(n * buf.shape[2], buf.shape[3])

    def edges(half, step):
        if half == 1:
            step(0)
            return

        def both(j, carry):
            step(j * (half - 1))
            return carry

        lax.fori_loop(0, 2, both, 0)

    def interior(half, step):
        def one_pair(j, carry):
            step(j)
            return carry

        if half > 2:
            lax.fori_loop(1, half - 1, one_pair, 0)

    def encode(src, weights, offset, dst, nxt, level, slot):
        half = (src.shape[1] - 2) // 2

        def step(i):
            made = []
            for h in range(hours):
                pair_of = conv(weights, offset, taps(src, h, 2 * i, 4), level)
                for off, row in enumerate(pair_of):
                    dst[h, 2 * i + off + 1] = row
                made += pair_of
            for h, row in enumerate(pooled(made)):
                nxt[h, i + 1] = row

        edges(half, step)
        wait = row_exchange(slot, nxt)
        interior(half, step)
        return wait

    def decode(low, up, skip, weights, offset, write, level, slot, sums, given):
        half = (skip.shape[1] - 2) // 2
        last, end = low.shape[1] - 2, skip.shape[1] - 2
        lanes = (LANES, far) if level is None else None

        def step(i, top=False, bottom=False):
            for h in range(hours):
                above, here, below = up[h, i], up[h, i + 1], up[h, i + 2]
                operand = jnp.concatenate(
                    (above, here, here, below, taps(skip, h, 2 * i, 4)), axis=0
                )
                more = (given[0, h] if top else None, given[1, h] if bottom else None)
                made = conv(weights, offset, operand, level, lanes, more)
                for off, row in enumerate(made):
                    write(h, 2 * i + off, row)

        widen(low, up, 1, last + 1)
        for h in range(hours):
            blank, empty = jnp.zeros_like(up[h, 1]), jnp.zeros_like(skip[h, 1])
            operand = jnp.concatenate(
                (up[h, last], blank, blank, up[h, 1])
                + (skip[h, end], empty, empty, skip[h, 1]),
                axis=0,
            )
            for at, total in enumerate(combined(weights, offset.shape[0], operand, lanes)):
                sums[at, h] = total.astype(jnp.bfloat16)
        wait = vertical(slot, sums.at[1], sums.at[0], given.at[1], given.at[0])
        interior(half, step)
        wait()
        if half == 1:
            step(0, True, True)
        else:
            step(0, True, False)
            step(half - 1, False, True)

    encode(f0, w1, v1, s1, p1, 0, 4)()
    encode(p1, w2, v2, s2, p2, 1, 5)()
    encode(p2, w3, v3, s3, p3, 2, 6)()
    for h in range(hours):
        for r in range(c4.shape[1] - 2):
            (c4[h, r + 1],) = conv(wc, vc, taps(p3, h, r, 3), 3)

    def keep(buf):
        def write(h, r, value):
            buf[h, r + 1] = value

        return write

    decode(c4, u3, s3, x3, y3, keep(b3), 2, 7, q3, g3)
    decode(b3, u2, s2, x2, y2, keep(b2), 1, 8, q2, g2)

    def head(h, r, value):
        total = jnp.dot(wh[...], value, preferred_element_type=jnp.float32)
        total = total + yh[...]
        out[h, r] = total + f0[h, r + 1, :, LANES:far].astype(jnp.float32)

    decode(b2, u1, s1, x1, y1, head, None, 9, q1, g1)


def narrow(depth, size):
    return size < LANES and size < depth


def body(nty, ntx, fields, *weights):
    hours, nv, rows, core = fields.shape
    sizes = [k.shape[3] for k in weights[0:8:2]]
    c1, c2, c3, c4 = sizes
    w1 = core + 2 * LANES
    w2 = halved(w1)
    w3 = halved(w2)
    w4 = halved(w3)
    r1, r2, r3, r4 = (rows + 2, rows // 2 + 2, rows // 4 + 2, rows // 8 + 2)
    shapes = (
        (hours, r1, nv, w1),
        (hours, r1, c1, w1),
        (hours, r2, c1, w2),
        (hours, r2, c2, w2),
        (hours, r3, c2, w3),
        (hours, r3, c3, w3),
        (hours, r4, c3, w4),
        (hours, r4, c4, w4),
        (hours, r4, c4, w3),
        (hours, r3, c3, w3),
        (hours, r3, c3, w2),
        (hours, r2, c2, w2),
        (hours, r2, c2, w1),
        (2 * LANES, LANES),
        (LANES, 2 * LANES),
        (6 * c1, 4 * nv),
        (6 * c2, 4 * c1),
        (6 * c3, 4 * c2),
        (3 * c4, 3 * c3),
        (6 * c3, 4 * (c4 + c3)),
        (6 * c2, 4 * (c3 + c2)),
        (6 * c1, 4 * (c2 + c1)),
        (nv, c1),
    )
    swapped = [
        jnp.swapaxes(k, 2, 3) if k.ndim == 4 and narrow(k.shape[2], k.shape[3]) else k
        for k in weights
    ]
    sums = [
        (2, hours, n, width)
        for n, width in ((c3, w3), (c2, w2), (c1, core))
        for _ in range(2)
    ]
    columns = (c1, c2, c3, c4, c3, c2, c1, nv)
    vmem = pl.BlockSpec(memory_space=pltpu.VMEM)
    result = pl.pallas_call(
        functools.partial(kernel, (nty, ntx)),
        out_shape=jax.ShapeDtypeStruct((hours, rows, nv, core), jnp.float32),
        in_specs=[vmem] * 17,
        out_specs=vmem,
        scratch_shapes=[pltpu.VMEM(shape, jnp.bfloat16) for shape in shapes]
        + [pltpu.VMEM((n, 1), jnp.float32) for n in columns]
        + [pltpu.VMEM(shape, jnp.bfloat16) for shape in sums]
        + [pltpu.SemaphoreType.DMA((20,)), pltpu.SemaphoreType.DMA((20,))],
        compiler_params=pltpu.CompilerParams(
            collective_id=0, has_side_effects=True, vmem_limit_bytes=56 * 2**20
        ),
    )(jnp.transpose(fields, (0, 2, 1, 3)), *swapped)
    return jnp.transpose(result, (0, 2, 1, 3))


def solution(mesh):
    return jax.shard_map(
        functools.partial(body, mesh.shape["ty"], mesh.shape["tx"]),
        mesh=mesh,
        in_specs=(P(None, None, "ty", "tx"),) + (P(),) * 16,
        out_specs=P(None, None, "ty", "tx"),
        check_vma=False,
    )
```

```python
import functools

import jax
import jax.numpy as jnp
from jax import lax
from jax.experimental import pallas as pl
from jax.experimental.pallas import tpu as pltpu
from jax.sharding import PartitionSpec as P

LANES = 128
MESH = pl.DeviceIdType.MESH


def halved(width):
    return -(-width // (2 * LANES)) * LANES


def kernel(
    sizes,
    fields,
    k1,
    o1,
    k2,
    o2,
    k3,
    o3,
    kc,
    oc,
    d3,
    e3,
    d2,
    e2,
    d1,
    e1,
    hk,
    he,
    out,
    f0,
    s1,
    p1,
    s2,
    p2,
    s3,
    p3,
    c4,
    u3,
    b3,
    u2,
    b2,
    u1,
    pool_m,
    up_m,
    w1,
    w2,
    w3,
    wc,
    x3,
    x2,
    x1,
    wh,
    v1,
    v2,
    v3,
    vc,
    y3,
    y2,
    y1,
    yh,
    q3,
    g3,
    q2,
    g2,
    q1,
    g1,
    send,
    recv,
):
    nty, ntx = sizes
    hours, rows, _, core = fields.shape
    ty, tx = lax.axis_index("ty"), lax.axis_index("tx")
    has_up, has_down = ty > 0, ty < nty - 1
    has_left, has_right = tx > 0, tx < ntx - 1
    far = LANES + core

    for buf in (f0, s1, p1, s2, p2, s3, p3, u3, u2, u1):
        edge = jnp.zeros((buf.shape[0],) + buf.shape[2:], buf.dtype)
        buf[:, 0] = edge
        buf[:, buf.shape[1] - 1] = edge
    for buf in (g3, g2, g1):
        buf[...] = jnp.zeros(buf.shape, buf.dtype)
    side = jnp.zeros((hours, rows) + (f0.shape[2], LANES), f0.dtype)
    f0[:, 1 : rows + 1, :, 0:LANES] = side
    f0[:, 1 : rows + 1, :, far : far + LANES] = side

    barrier = pltpu.get_barrier_semaphore()
    sides = (
        (has_up, {"ty": ty - 1}),
        (has_down, {"ty": ty + 1}),
        (has_left, {"tx": tx - 1}),
        (has_right, {"tx": tx + 1}),
    )
    count = jnp.int32(0)
    for has, where in sides:
        count = count + jnp.where(has, 1, 0)

        @pl.when(has)
        def _():
            pl.semaphore_signal(barrier, inc=1, device_id=where, device_id_type=MESH)

    pl.semaphore_wait(barrier, count)

    slots = iter(range(send.shape[0] // 2))

    def pair(first, second):
        made, slot = [], next(slots)
        for at, (has, other, where, src, dst) in enumerate((first, second)):
            copy = pltpu.make_async_remote_copy(
                src_ref=src,
                dst_ref=dst,
                send_sem=send.at[slot * 2 + at],
                recv_sem=recv.at[slot * 2 + at],
                device_id=where,
                device_id_type=MESH,
            )
            made.append((has, other, copy))

            @pl.when(has)
            def _():
                copy.start()

        def wait():
            for has, other, copy in made:

                @pl.when(has)
                def _():
                    copy.wait_send()

                @pl.when(other)
                def _():
                    copy.wait_recv()

        return wait

    def vertical(top, bottom, after, before):
        return pair(
            (has_up, has_down, {"ty": ty - 1}, top, after),
            (has_down, has_up, {"ty": ty + 1}, bottom, before),
        )

    def row_exchange(buf, h):
        last = buf.shape[1] - 1
        return vertical(buf.at[h, 1], buf.at[h, last - 1], buf.at[h, last], buf.at[h, 0])

    def column_exchange(h):
        return pair(
            (
                has_left,
                has_right,
                {"tx": tx - 1},
                fields.at[h, :, :, pl.ds(0, LANES)],
                f0.at[h, pl.ds(1, rows), :, pl.ds(far, LANES)],
            ),
            (
                has_right,
                has_left,
                {"tx": tx + 1},
                fields.at[h, :, :, pl.ds(core - LANES, LANES)],
                f0.at[h, pl.ds(1, rows), :, pl.ds(0, LANES)],
            ),
        )

    middle = pl.ds(LANES, core)
    wait_sides = [column_exchange(h) for h in range(hours)]
    wait_rows = [
        vertical(
            fields.at[h, 0],
            fields.at[h, rows - 1],
            f0.at[h, rows + 1, :, middle],
            f0.at[h, 0, :, middle],
        )
        for h in range(hours)
    ]

    f0[:, 1 : rows + 1, :, LANES:far] = fields[...]
    two, one = 2 * LANES, LANES
    tall = lax.broadcasted_iota(jnp.int32, (two, one), 0)
    wide = lax.broadcasted_iota(jnp.int32, (two, one), 1)
    pool_m[...] = jnp.where(lax.shift_right_logical(tall, 1) == wide, 0.25, 0.0).astype(jnp.bfloat16)
    tall = lax.broadcasted_iota(jnp.int32, (one, two), 0)
    wide = lax.broadcasted_iota(jnp.int32, (one, two), 1)
    up_m[...] = jnp.where(lax.shift_right_logical(wide, 1) == tall, 1.0, 0.0).astype(jnp.bfloat16)

    def eye(n):
        down = lax.broadcasted_iota(jnp.int32, (n, n), 0)
        across = lax.broadcasted_iota(jnp.int32, (n, n), 1)
        return down == across

    def turned(block):
        return lax.dot_general(
            jnp.where(eye(block.shape[1]), 1.0, 0.0).astype(jnp.bfloat16),
            block,
            (((1,), (1,)), ((), ())),
            preferred_element_type=jnp.float32,
        ).astype(jnp.bfloat16)

    def arrange(src, dst, cuts):
        straight = src.shape[2] == cuts[-1][1]
        size = src.shape[3] if straight else src.shape[2]
        count = dst.shape[0] // (3 * size)
        for c in range(3):
            if straight:
                rows_of = src[:, c]
            else:
                rows_of = jnp.stack([turned(src[a, c]) for a in range(3)])
            for off in range(count):
                blocks = []
                for start, stop in cuts:
                    zero = jnp.zeros((stop - start, size), jnp.bfloat16)
                    taken = rows_of[:, start:stop].reshape(3 * (stop - start), size)
                    blocks += [zero] * off + [taken] + [zero] * (count - 1 - off)
                block = blocks[0] if len(blocks) == 1 else jnp.concatenate(blocks, axis=0)
                at = (off * 3 + c) * size
                dst[at : at + size] = turned(block)

    def upright(src, dst):
        n = src.shape[0]
        row = jnp.broadcast_to(src[...].reshape(1, n), (n, n))
        dst[...] = jnp.sum(jnp.where(eye(n), row, 0.0), axis=1, keepdims=True)

    def inside(width, level):
        column = lax.broadcasted_iota(jnp.int32, (1, width), 1)
        column = column + (tx * (core >> level) - (LANES >> level))
        return (column >= 0) & (column < ntx * (core >> level))

    def combined(weights, size, operand, lanes):
        width = operand.shape[1]
        terms = jnp.dot(weights[...], operand, preferred_element_type=jnp.float32)
        made = []
        for at in range(0, terms.shape[0], 3 * size):
            total = terms[at + size : at + 2 * size]
            total = total + pltpu.roll(terms[at : at + size], 1, 1)
            total = total + pltpu.roll(terms[at + 2 * size : at + 3 * size], width - 1, 1)
            made.append(total if lanes is None else total[:, lanes[0] : lanes[1]])
        return made

    def conv(weights, offset, operand, level, lanes=None, more=(None, None)):
        made = []
        for total, extra in zip(combined(weights, offset.shape[0], operand, lanes), more):
            total = total + offset[...]
            if extra is not None:
                total = total + extra.astype(jnp.float32)
            half = 0.5 * total
            result = half * jnp.tanh(half) + half
            if level is not None:
                result = jnp.where(inside(result.shape[1], level), result, 0.0)
            made.append(result.astype(jnp.bfloat16))
        return made

    def pooled(values):
        width = values[0].shape[1]
        size = values[0].shape[0]
        tall = jnp.concatenate(values, axis=0)
        pieces = []
        for start in range(0, width, two):
            stop = min(start + two, width)
            pieces.append(
                jnp.dot(tall[:, start:stop], pool_m[0 : stop - start], preferred_element_type=jnp.float32)
            )
        sums = jnp.concatenate(pieces, axis=1)
        return [
            (sums[at : at + size] + sums[at + size : at + 2 * size]).astype(jnp.bfloat16)
            for at in range(0, size * len(values), 2 * size)
        ]

    def widen(src, dst, h, first, last):
        width = dst.shape[3]
        size = src.shape[2]
        n = last - first
        for start in range(0, width, two):
            stop = min(start + two, width)
            block = src[h, first:last, :, start // 2 : start // 2 + one]
            wide = jnp.dot(
                block.reshape(n * size, one),
                up_m[:, 0 : stop - start],
                preferred_element_type=jnp.float32,
            ).astype(jnp.bfloat16)
            dst[h, first:last, :, start:stop] = wide.reshape(n, size, stop - start)

    def taps(buf, h, r, n):
        block = buf[h, pl.ds(r, n)]
        return block.reshape(n * buf.shape[2], buf.shape[3])

    def interior(half, step):
        def one_pair(j, carry):
            step(j)
            return carry

        if half > 2:
            lax.fori_loop(1, half - 1, one_pair, 0)

    def encoder(src, weights, offset, dst, nxt, level):
        half = (src.shape[1] - 2) // 2

        def inner(h):
            def step(i):
                made = conv(weights, offset, taps(src, h, 2 * i, 4), level)
                for off, row in enumerate(made):
                    dst[h, 2 * i + off + 1] = row
                (nxt[h, i + 1],) = pooled(made)

            return step

        def outer(h):
            for i in sorted({0, half - 1}):
                inner(h)(i)
            return row_exchange(nxt, h)

        return lambda h: interior(half, inner(h)), outer

    def decoder(low, up, skip, weights, offset, write, level, sums, given):
        half = (skip.shape[1] - 2) // 2
        last, end = low.shape[1] - 2, skip.shape[1] - 2
        lanes = (LANES, far) if level is None else None

        def inner(h, top=False, bottom=False):
            def step(i):
                above, here, below = up[h, i], up[h, i + 1], up[h, i + 2]
                operand = jnp.concatenate(
                    (above, here, here, below, taps(skip, h, 2 * i, 4)), axis=0
                )
                more = (given[0, h] if top else None, given[1, h] if bottom else None)
                made = conv(weights, offset, operand, level, lanes, more)
                for off, row in enumerate(made):
                    write(h, 2 * i + off, row)

            return step

        def begin(h):
            widen(low, up, h, 1, last + 1)
            blank, empty = jnp.zeros_like(up[h, 1]), jnp.zeros_like(skip[h, 1])
            operand = jnp.concatenate(
                (up[h, last], blank, blank, up[h, 1])
                + (skip[h, end], empty, empty, skip[h, 1]),
                axis=0,
            )
            for at, total in enumerate(combined(weights, offset.shape[0], operand, lanes)):
                sums[at, h] = total.astype(jnp.bfloat16)
            return vertical(sums.at[1, h], sums.at[0, h], given.at[1, h], given.at[0, h])

        def finish(h):
            for i in sorted({0, half - 1}):
                inner(h, i == 0, i == half - 1)(i)

        return begin, lambda h: interior(half, inner(h)), finish

    def keep(buf):
        def write(h, r, value):
            buf[h, r + 1] = value

        return write

    def head(h, r, value):
        total = jnp.dot(wh[...], value, preferred_element_type=jnp.float32)
        total = total + yh[...]
        out[h, r] = total + f0[h, r + 1, :, LANES:far].astype(jnp.float32)

    def encoder_weights(src, dst, buf):
        arrange(src, dst, ((0, buf.shape[2]),))

    def decoder_weights(src, dst, low, skip):
        cut = low.shape[2]
        arrange(src, dst, ((0, cut), (cut, cut + skip.shape[2])))

    each = range(hours)
    inner_one, outer_one = encoder(f0, w1, v1, s1, p1, 0)
    inner_two, outer_two = encoder(p1, w2, v2, s2, p2, 1)
    inner_three, outer_three = encoder(p2, w3, v3, s3, p3, 2)
    begin_three, center_three, finish_three = decoder(
        c4, u3, s3, x3, y3, keep(b3), 2, q3, g3
    )
    begin_two, center_two, finish_two = decoder(b3, u2, s2, x2, y2, keep(b2), 1, q2, g2)
    begin_one, center_one, finish_one = decoder(b2, u1, s1, x1, y1, head, None, q1, g1)

    encoder_weights(k1, w1, f0)
    for src, dst in zip((o1, o2, o3, oc, e3, e2, e1, he), (v1, v2, v3, vc, y3, y2, y1, yh)):
        upright(src, dst)
    corners = []
    for h in each:
        wait_sides[h]()
        for start in (0, far):
            lanes_of = pl.ds(start, LANES)
            corners.append(
                vertical(
                    f0.at[h, 1, :, lanes_of],
                    f0.at[h, rows, :, lanes_of],
                    f0.at[h, rows + 1, :, lanes_of],
                    f0.at[h, 0, :, lanes_of],
                )
            )
    for h in each:
        inner_one(h)
    encoder_weights(k2, w2, p1)
    waits = []
    for h in each:
        wait_rows[h]()
        corners[2 * h]()
        corners[2 * h + 1]()
        waits.append(outer_one(h))
    encoder_weights(k3, w3, p2)
    encoder_weights(kc, wc, p3)
    decoder_weights(d1, x1, b2, s1)

    def after(waits, work):
        made = []
        for h in each:
            waits[h]()
            made.append(work(h))
        return made

    def second(h):
        inner_two(h)
        return outer_two(h)

    def third(h):
        inner_three(h)
        return outer_three(h)

    def fourth(h):
        for r in range(c4.shape[1] - 2):
            (c4[h, r + 1],) = conv(wc, vc, taps(p3, h, r, 3), 3)
        return begin_three(h)

    def fifth(h):
        finish_three(h)
        return begin_two(h)

    def sixth(h):
        finish_two(h)
        return begin_one(h)

    waits = after(waits, second)
    decoder_weights(d2, x2, b3, s2)
    waits = after(waits, third)
    decoder_weights(d3, x3, c4, s3)
    wh[...] = turned(hk[...])
    waits = after(waits, fourth)
    for h in each:
        center_three(h)
    waits = after(waits, fifth)
    for h in each:
        center_two(h)
    waits = after(waits, sixth)
    for h in each:
        center_one(h)
    after(waits, finish_one)


def narrow(depth, size):
    return size < LANES and size < depth


def body(nty, ntx, fields, *weights):
    hours, nv, rows, core = fields.shape
    sizes = [k.shape[3] for k in weights[0:8:2]]
    c1, c2, c3, c4 = sizes
    w1 = core + 2 * LANES
    w2 = halved(w1)
    w3 = halved(w2)
    w4 = halved(w3)
    r1, r2, r3, r4 = (rows + 2, rows // 2 + 2, rows // 4 + 2, rows // 8 + 2)
    shapes = (
        (hours, r1, nv, w1),
        (hours, r1, c1, w1),
        (hours, r2, c1, w2),
        (hours, r2, c2, w2),
        (hours, r3, c2, w3),
        (hours, r3, c3, w3),
        (hours, r4, c3, w4),
        (hours, r4, c4, w4),
        (hours, r4, c4, w3),
        (hours, r3, c3, w3),
        (hours, r3, c3, w2),
        (hours, r2, c2, w2),
        (hours, r2, c2, w1),
        (2 * LANES, LANES),
        (LANES, 2 * LANES),
        (6 * c1, 4 * nv),
        (6 * c2, 4 * c1),
        (6 * c3, 4 * c2),
        (3 * c4, 3 * c3),
        (6 * c3, 4 * (c4 + c3)),
        (6 * c2, 4 * (c3 + c2)),
        (6 * c1, 4 * (c2 + c1)),
        (nv, c1),
    )
    swapped = [
        jnp.swapaxes(k, 2, 3) if k.ndim == 4 and narrow(k.shape[2], k.shape[3]) else k
        for k in weights
    ]
    sums = [
        (2, hours, n, width)
        for n, width in ((c3, w3), (c2, w2), (c1, core))
        for _ in range(2)
    ]
    columns = (c1, c2, c3, c4, c3, c2, c1, nv)
    vmem = pl.BlockSpec(memory_space=pltpu.VMEM)
    result = pl.pallas_call(
        functools.partial(kernel, (nty, ntx)),
        out_shape=jax.ShapeDtypeStruct((hours, rows, nv, core), jnp.float32),
        in_specs=[vmem] * 17,
        out_specs=vmem,
        scratch_shapes=[pltpu.VMEM(shape, jnp.bfloat16) for shape in shapes]
        + [pltpu.VMEM((n, 1), jnp.float32) for n in columns]
        + [pltpu.VMEM(shape, jnp.bfloat16) for shape in sums]
        + [pltpu.SemaphoreType.DMA((20 * hours,))] * 2,
        compiler_params=pltpu.CompilerParams(
            collective_id=0, has_side_effects=True, vmem_limit_bytes=56 * 2**20
        ),
    )(jnp.transpose(fields, (0, 2, 1, 3)), *swapped)
    return jnp.transpose(result, (0, 2, 1, 3))


def solution(mesh):
    return jax.shard_map(
        functools.partial(body, mesh.shape["ty"], mesh.shape["tx"]),
        mesh=mesh,
        in_specs=(P(None, None, "ty", "tx"),) + (P(),) * 16,
        out_specs=P(None, None, "ty", "tx"),
        check_vma=False,
    )
```

```python
import functools

import jax
import jax.numpy as jnp
from jax import lax
from jax.experimental import pallas as pl
from jax.experimental.pallas import tpu as pltpu
from jax.sharding import PartitionSpec as P

LANES = 128
MESH = pl.DeviceIdType.MESH


def halved(width):
    return -(-width // (2 * LANES)) * LANES


def kernel(
    sizes,
    fields,
    k1,
    o1,
    k2,
    o2,
    k3,
    o3,
    kc,
    oc,
    d3,
    e3,
    d2,
    e2,
    d1,
    e1,
    hk,
    he,
    out,
    f0,
    s1,
    p1,
    s2,
    p2,
    s3,
    p3,
    c4,
    u3,
    b3,
    u2,
    b2,
    u1,
    pool_m,
    up_m,
    w1,
    w2,
    w3,
    wc,
    x3,
    x2,
    x1,
    wh,
    v1,
    v2,
    v3,
    vc,
    y3,
    y2,
    y1,
    yh,
    q3,
    g3,
    q2,
    g2,
    q1,
    g1,
    send,
    recv,
):
    nty, ntx = sizes
    hours, rows, _, core = fields.shape
    ty, tx = lax.axis_index("ty"), lax.axis_index("tx")
    has_up, has_down = ty > 0, ty < nty - 1
    has_left, has_right = tx > 0, tx < ntx - 1
    far = LANES + core

    for buf in (f0, s1, p1, s2, p2, s3, p3, u3, u2, u1):
        edge = jnp.zeros((buf.shape[0],) + buf.shape[2:], buf.dtype)
        buf[:, 0] = edge
        buf[:, buf.shape[1] - 1] = edge
    for buf in (g3, g2, g1):
        buf[...] = jnp.zeros(buf.shape, buf.dtype)
    side = jnp.zeros((hours, rows) + (f0.shape[2], LANES), f0.dtype)
    f0[:, 1 : rows + 1, :, 0:LANES] = side
    f0[:, 1 : rows + 1, :, far : far + LANES] = side

    barrier = pltpu.get_barrier_semaphore()
    sides = (
        (has_up, {"ty": ty - 1}),
        (has_down, {"ty": ty + 1}),
        (has_left, {"tx": tx - 1}),
        (has_right, {"tx": tx + 1}),
    )
    count = jnp.int32(0)
    for has, where in sides:
        count = count + jnp.where(has, 1, 0)

        @pl.when(has)
        def _():
            pl.semaphore_signal(barrier, inc=1, device_id=where, device_id_type=MESH)

    pl.semaphore_wait(barrier, count)

    slots = iter(range(send.shape[0] // 2))

    def pair(first, second):
        made, slot = [], next(slots)
        for at, (has, other, where, src, dst) in enumerate((first, second)):
            copy = pltpu.make_async_remote_copy(
                src_ref=src,
                dst_ref=dst,
                send_sem=send.at[slot * 2 + at],
                recv_sem=recv.at[slot * 2 + at],
                device_id=where,
                device_id_type=MESH,
            )
            made.append((has, other, copy))

            @pl.when(has)
            def _():
                copy.start()

        def wait():
            for has, other, copy in made:

                @pl.when(has)
                def _():
                    copy.wait_send()

                @pl.when(other)
                def _():
                    copy.wait_recv()

        return wait

    def vertical(top, bottom, after, before):
        return pair(
            (has_up, has_down, {"ty": ty - 1}, top, after),
            (has_down, has_up, {"ty": ty + 1}, bottom, before),
        )

    def row_exchange(buf, h):
        last = buf.shape[1] - 1
        return vertical(buf.at[h, 1], buf.at[h, last - 1], buf.at[h, last], buf.at[h, 0])

    def column_exchange(h):
        return pair(
            (
                has_left,
                has_right,
                {"tx": tx - 1},
                fields.at[h, :, :, pl.ds(0, LANES)],
                f0.at[h, pl.ds(1, rows), :, pl.ds(far, LANES)],
            ),
            (
                has_right,
                has_left,
                {"tx": tx + 1},
                fields.at[h, :, :, pl.ds(core - LANES, LANES)],
                f0.at[h, pl.ds(1, rows), :, pl.ds(0, LANES)],
            ),
        )

    middle = pl.ds(LANES, core)
    wait_sides = [column_exchange(h) for h in range(hours)]
    wait_rows = [
        vertical(
            fields.at[h, 0],
            fields.at[h, rows - 1],
            f0.at[h, rows + 1, :, middle],
            f0.at[h, 0, :, middle],
        )
        for h in range(hours)
    ]

    f0[:, 1 : rows + 1, :, LANES:far] = fields[...]
    two, one = 2 * LANES, LANES
    tall = lax.broadcasted_iota(jnp.int32, (two, one), 0)
    wide = lax.broadcasted_iota(jnp.int32, (two, one), 1)
    pool_m[...] = jnp.where(lax.shift_right_logical(tall, 1) == wide, 0.25, 0.0).astype(jnp.bfloat16)
    tall = lax.broadcasted_iota(jnp.int32, (one, two), 0)
    wide = lax.broadcasted_iota(jnp.int32, (one, two), 1)
    up_m[...] = jnp.where(lax.shift_right_logical(wide, 1) == tall, 1.0, 0.0).astype(jnp.bfloat16)

    def eye(n):
        down = lax.broadcasted_iota(jnp.int32, (n, n), 0)
        across = lax.broadcasted_iota(jnp.int32, (n, n), 1)
        return down == across

    def turned(block):
        return lax.dot_general(
            jnp.where(eye(block.shape[1]), 1.0, 0.0).astype(jnp.bfloat16),
            block,
            (((1,), (1,)), ((), ())),
            preferred_element_type=jnp.float32,
        ).astype(jnp.bfloat16)

    def arrange(src, dst, cuts):
        straight = src.shape[2] == cuts[-1][1]
        size = src.shape[3] if straight else src.shape[2]
        count = dst.shape[0] // (3 * size)
        for c in range(3):
            if straight:
                rows_of = src[:, c]
            else:
                rows_of = jnp.stack([turned(src[a, c]) for a in range(3)])
            for off in range(count):
                blocks = []
                for start, stop in cuts:
                    zero = jnp.zeros((stop - start, size), jnp.bfloat16)
                    taken = rows_of[:, start:stop].reshape(3 * (stop - start), size)
                    blocks += [zero] * off + [taken] + [zero] * (count - 1 - off)
                block = blocks[0] if len(blocks) == 1 else jnp.concatenate(blocks, axis=0)
                at = (off * 3 + c) * size
                dst[at : at + size] = turned(block)

    def upright(src, dst):
        n = src.shape[0]
        row = jnp.broadcast_to(src[...].reshape(1, n), (n, n))
        dst[...] = jnp.sum(jnp.where(eye(n), row, 0.0), axis=1, keepdims=True)

    def inside(width, level):
        column = lax.broadcasted_iota(jnp.int32, (1, width), 1)
        column = column + (tx * (core >> level) - (LANES >> level))
        return (column >= 0) & (column < ntx * (core >> level))

    def combined(weights, size, operand, lanes):
        width = operand.shape[1]
        terms = jnp.dot(weights[...], operand, preferred_element_type=jnp.float32)
        made = []
        for at in range(0, terms.shape[0], 3 * size):
            total = terms[at + size : at + 2 * size]
            total = total + pltpu.roll(terms[at : at + size], 1, 1)
            total = total + pltpu.roll(terms[at + 2 * size : at + 3 * size], width - 1, 1)
            made.append(total if lanes is None else total[:, lanes[0] : lanes[1]])
        return made

    def conv(weights, offset, operand, level, lanes=None, more=(None, None)):
        made = []
        for total, extra in zip(combined(weights, offset.shape[0], operand, lanes), more):
            total = total + offset[...]
            if extra is not None:
                total = total + extra.astype(jnp.float32)
            half = 0.5 * total
            result = half * jnp.tanh(half) + half
            if level is not None:
                result = jnp.where(inside(result.shape[1], level), result, 0.0)
            made.append(result.astype(jnp.bfloat16))
        return made

    def pooled(values):
        width = values[0].shape[1]
        size = values[0].shape[0]
        tall = jnp.concatenate(values, axis=0)
        pieces = []
        for start in range(0, width, two):
            stop = min(start + two, width)
            pieces.append(
                jnp.dot(tall[:, start:stop], pool_m[0 : stop - start], preferred_element_type=jnp.float32)
            )
        sums = jnp.concatenate(pieces, axis=1)
        return [
            (sums[at : at + size] + sums[at + size : at + 2 * size]).astype(jnp.bfloat16)
            for at in range(0, size * len(values), 2 * size)
        ]

    def widen(src, dst, h, first, last):
        width = dst.shape[3]
        size = src.shape[2]
        n = last - first
        for start in range(0, width, two):
            stop = min(start + two, width)
            block = src[h, first:last, :, start // 2 : start // 2 + one]
            wide = jnp.dot(
                block.reshape(n * size, one),
                up_m[:, 0 : stop - start],
                preferred_element_type=jnp.float32,
            ).astype(jnp.bfloat16)
            dst[h, first:last, :, start:stop] = wide.reshape(n, size, stop - start)

    def taps(buf, h, r, n):
        block = buf[h, pl.ds(r, n)]
        return block.reshape(n * buf.shape[2], buf.shape[3])

    def interior(half, step):
        def one_pair(j, carry):
            step(j)
            return carry

        if half > 2:
            lax.fori_loop(1, half - 1, one_pair, 0)

    def encoder(src, weights, offset, dst, nxt, level):
        half = (src.shape[1] - 2) // 2

        def inner(h):
            def step(i):
                made = conv(weights, offset, taps(src, h, 2 * i, 4), level)
                for off, row in enumerate(made):
                    dst[h, 2 * i + off + 1] = row
                (nxt[h, i + 1],) = pooled(made)

            return step

        def outer(h):
            for i in sorted({0, half - 1}):
                inner(h)(i)
            return row_exchange(nxt, h)

        return lambda h: interior(half, inner(h)), outer

    def decoder(low, up, skip, weights, offset, write, level, sums, given):
        half = (skip.shape[1] - 2) // 2
        last, end = low.shape[1] - 2, skip.shape[1] - 2
        lanes = (LANES, far) if level is None else None

        def inner(h, top=False, bottom=False):
            def step(i):
                above, here, below = up[h, i], up[h, i + 1], up[h, i + 2]
                operand = jnp.concatenate(
                    (above, here, here, below, taps(skip, h, 2 * i, 4)), axis=0
                )
                more = (given[0, h] if top else None, given[1, h] if bottom else None)
                made = conv(weights, offset, operand, level, lanes, more)
                for off, row in enumerate(made):
                    write(h, 2 * i + off, row)

            return step

        def begin(h):
            widen(low, up, h, 1, last + 1)
            n, m, size = up.shape[2], skip.shape[2], offset.shape[0]
            if n % LANES == 0 and m % LANES == 0:
                for at, r, s in ((0, last, end), (1, 1, 1)):
                    band = slice(3 * size * at, 3 * size * (at + 1))
                    first, other = 3 * n * at, 4 * n + 3 * m * at
                    taken = jnp.concatenate(
                        (weights[band, first : first + n], weights[band, other : other + m]),
                        axis=1,
                    )
                    row = jnp.concatenate((up[h, r], skip[h, s]), axis=0)
                    (total,) = combined(taken, size, row, lanes)
                    sums[at, h] = total.astype(jnp.bfloat16)
                return vertical(sums.at[1, h], sums.at[0, h], given.at[1, h], given.at[0, h])
            blank, empty = jnp.zeros_like(up[h, 1]), jnp.zeros_like(skip[h, 1])
            operand = jnp.concatenate(
                (up[h, last], blank, blank, up[h, 1])
                + (skip[h, end], empty, empty, skip[h, 1]),
                axis=0,
            )
            for at, total in enumerate(combined(weights, offset.shape[0], operand, lanes)):
                sums[at, h] = total.astype(jnp.bfloat16)
            return vertical(sums.at[1, h], sums.at[0, h], given.at[1, h], given.at[0, h])

        def finish(h):
            for i in sorted({0, half - 1}):
                inner(h, i == 0, i == half - 1)(i)

        return begin, lambda h: interior(half, inner(h)), finish

    def keep(buf):
        def write(h, r, value):
            buf[h, r + 1] = value

        return write

    def head(h, r, value):
        total = jnp.dot(wh[...], value, preferred_element_type=jnp.float32)
        total = total + yh[...]
        out[h, r] = total + f0[h, r + 1, :, LANES:far].astype(jnp.float32)

    def encoder_weights(src, dst, buf):
        arrange(src, dst, ((0, buf.shape[2]),))

    def decoder_weights(src, dst, low, skip):
        cut = low.shape[2]
        arrange(src, dst, ((0, cut), (cut, cut + skip.shape[2])))

    each = range(hours)
    inner_one, outer_one = encoder(f0, w1, v1, s1, p1, 0)
    inner_two, outer_two = encoder(p1, w2, v2, s2, p2, 1)
    inner_three, outer_three = encoder(p2, w3, v3, s3, p3, 2)
    begin_three, center_three, finish_three = decoder(
        c4, u3, s3, x3, y3, keep(b3), 2, q3, g3
    )
    begin_two, center_two, finish_two = decoder(b3, u2, s2, x2, y2, keep(b2), 1, q2, g2)
    begin_one, center_one, finish_one = decoder(b2, u1, s1, x1, y1, head, None, q1, g1)

    encoder_weights(k1, w1, f0)
    for src, dst in zip((o1, o2, o3, oc, e3, e2, e1, he), (v1, v2, v3, vc, y3, y2, y1, yh)):
        upright(src, dst)
    corners = []
    for h in each:
        wait_sides[h]()
        for start in (0, far):
            lanes_of = pl.ds(start, LANES)
            corners.append(
                vertical(
                    f0.at[h, 1, :, lanes_of],
                    f0.at[h, rows, :, lanes_of],
                    f0.at[h, rows + 1, :, lanes_of],
                    f0.at[h, 0, :, lanes_of],
                )
            )
    for h in each:
        inner_one(h)
    encoder_weights(k2, w2, p1)
    waits = []
    for h in each:
        wait_rows[h]()
        corners[2 * h]()
        corners[2 * h + 1]()
        waits.append(outer_one(h))
    encoder_weights(k3, w3, p2)
    encoder_weights(kc, wc, p3)
    decoder_weights(d1, x1, b2, s1)

    def after(waits, work):
        made = []
        for h in each:
            waits[h]()
            made.append(work(h))
        return made

    def second(h):
        inner_two(h)
        return outer_two(h)

    def third(h):
        inner_three(h)
        return outer_three(h)

    def fourth(h):
        for r in range(c4.shape[1] - 2):
            (c4[h, r + 1],) = conv(wc, vc, taps(p3, h, r, 3), 3)
        return begin_three(h)

    def fifth(h):
        finish_three(h)
        return begin_two(h)

    def sixth(h):
        finish_two(h)
        return begin_one(h)

    waits = after(waits, second)
    decoder_weights(d2, x2, b3, s2)
    waits = after(waits, third)
    decoder_weights(d3, x3, c4, s3)
    wh[...] = turned(hk[...])
    waits = after(waits, fourth)
    for h in each:
        center_three(h)
    waits = after(waits, fifth)
    for h in each:
        center_two(h)
    waits = after(waits, sixth)
    for h in each:
        center_one(h)
    after(waits, finish_one)


def narrow(depth, size):
    return size < LANES and size < depth


def body(nty, ntx, fields, *weights):
    hours, nv, rows, core = fields.shape
    sizes = [k.shape[3] for k in weights[0:8:2]]
    c1, c2, c3, c4 = sizes
    w1 = core + 2 * LANES
    w2 = halved(w1)
    w3 = halved(w2)
    w4 = halved(w3)
    r1, r2, r3, r4 = (rows + 2, rows // 2 + 2, rows // 4 + 2, rows // 8 + 2)
    shapes = (
        (hours, r1, nv, w1),
        (hours, r1, c1, w1),
        (hours, r2, c1, w2),
        (hours, r2, c2, w2),
        (hours, r3, c2, w3),
        (hours, r3, c3, w3),
        (hours, r4, c3, w4),
        (hours, r4, c4, w4),
        (hours, r4, c4, w3),
        (hours, r3, c3, w3),
        (hours, r3, c3, w2),
        (hours, r2, c2, w2),
        (hours, r2, c2, w1),
        (2 * LANES, LANES),
        (LANES, 2 * LANES),
        (6 * c1, 4 * nv),
        (6 * c2, 4 * c1),
        (6 * c3, 4 * c2),
        (3 * c4, 3 * c3),
        (6 * c3, 4 * (c4 + c3)),
        (6 * c2, 4 * (c3 + c2)),
        (6 * c1, 4 * (c2 + c1)),
        (nv, c1),
    )
    swapped = [
        jnp.swapaxes(k, 2, 3) if k.ndim == 4 and narrow(k.shape[2], k.shape[3]) else k
        for k in weights
    ]
    sums = [
        (2, hours, n, width)
        for n, width in ((c3, w3), (c2, w2), (c1, core))
        for _ in range(2)
    ]
    columns = (c1, c2, c3, c4, c3, c2, c1, nv)
    vmem = pl.BlockSpec(memory_space=pltpu.VMEM)
    result = pl.pallas_call(
        functools.partial(kernel, (nty, ntx)),
        out_shape=jax.ShapeDtypeStruct((hours, rows, nv, core), jnp.float32),
        in_specs=[vmem] * 17,
        out_specs=vmem,
        scratch_shapes=[pltpu.VMEM(shape, jnp.bfloat16) for shape in shapes]
        + [pltpu.VMEM((n, 1), jnp.float32) for n in columns]
        + [pltpu.VMEM(shape, jnp.bfloat16) for shape in sums]
        + [pltpu.SemaphoreType.DMA((20 * hours,))] * 2,
        compiler_params=pltpu.CompilerParams(
            collective_id=0, has_side_effects=True, vmem_limit_bytes=56 * 2**20
        ),
    )(jnp.transpose(fields, (0, 2, 1, 3)), *swapped)
    return jnp.transpose(result, (0, 2, 1, 3))


def solution(mesh):
    return jax.shard_map(
        functools.partial(body, mesh.shape["ty"], mesh.shape["tx"]),
        mesh=mesh,
        in_specs=(P(None, None, "ty", "tx"),) + (P(),) * 16,
        out_specs=P(None, None, "ty", "tx"),
        check_vma=False,
    )
```
